512 devices in a mesh: pos: 32 (over z, core), trk: 16 (over y, x).
Axes of the slice: x: 4, y: 4, z: 16, core: 2. Of those that a mesh axis runs over, the one named last changes fastest.
Arguments:
- activations: bfloat16 [4, 16384, 1536], P(None, 'pos', 'trk'), may hold values from -6 to 6
- norm_gain: float32 [1536], P('trk'), may hold values from 0.1 to 1.9
- norm_bias: float32 [1536], P('trk'), may hold values from -1 to 1
- conv_weight: bfloat16 [3, 1536, 1536], P(None, None, 'trk'), may hold values from -0.09375 to 0.09375
- head_weight: bfloat16 [1536, 4096], P(None, 'trk'), may hold values from -0.15625 to 0.15625
- head_bias: float32 [4096], P('trk'), may hold values from -2 to 0
- gene_slot: int32 [4, 16384], P(None, 'pos'), may hold values from -1 to 35, as said below
- straddle_map: int32 [128], P('pos'), may hold values from -1 to 31, as said below
Outputs:
- tracks: bfloat16 [4, 16384, 4096], P(None, 'pos', 'trk')
- gene_mean: float32 [1024, 4096], P('pos', 'trk')
The draws below stay inside these ranges and needn't reach their ends.
Inputs may be any that keep to these rules, and one draw needn't show every extreme that they name: `gene_slot`: -1 marks a bin outside exons. A value g below 32 names gene g of the bin's own block of 512 positions; 32 + s names entry s of the previous block's straddle list and appears only where that entry is not -1, never in the first block. `straddle_map`: entry index * 4 + s names the gene of block index that entry s of its straddle list stands for, or -1; the live entries of one block are distinct, and the last block's are all -1.
All inputs are finite; a program needn't handle non-finite values.
Results may differ from the reference program's by a relative error of at most 0.0048.
Values may be sent and summed in bfloat16 or wider, within the bound.
A program may use at most 128 MiB of HBM per device.

```python
import jax
import jax.numpy as jnp
from jax import lax

SEQS = 4
POS_DEV = 512
C = 1536
TRACKS = 4096
GENES_DEV = 32
STRAD = 4
LEN = 16384
GENES = 1024
N_POS = 32


def gene_layout(key):
    base = jax.random.fold_in(key, 4099)
    key_flag, key_keep, key_exon = jax.random.split(base, 3)
    windows = GENES_DEV // SEQS
    span = POS_DEV // windows
    flags = jax.random.randint(key_flag, (N_POS, SEQS), 0, 2)
    not_last = (jnp.arange(N_POS) < N_POS - 1).astype(jnp.int32)
    flags = flags * not_last[:, None]
    keeping = jax.random.randint(key_keep, (N_POS, SEQS, windows), 0, 8) > 0
    exonic = jax.random.randint(key_exon, (N_POS, SEQS, POS_DEV), 0, 2) > 0
    offsets = jnp.arange(POS_DEV)
    window = offsets // span
    seq_ids = jnp.arange(SEQS)
    own_slot = seq_ids[None, :, None] * windows + window[None, None, :]
    forced = (window[None, None, :] == windows - 1) & (flags[:, :, None] > 0)
    alive = keeping[:, :, window] | forced
    previous = jnp.concatenate([jnp.zeros((1, SEQS), jnp.int32), flags[:-1]], axis=0)
    entering = (offsets[None, None, :] < span // 2) & (previous[:, :, None] > 0)
    slot_ids = jnp.where(entering, GENES_DEV + seq_ids[None, :, None], jnp.where(alive, own_slot, -1))
    slot_ids = jnp.where(exonic, slot_ids, -1)
    gene_slot = jnp.transpose(slot_ids, (1, 0, 2)).reshape(SEQS, N_POS * POS_DEV)
    straddle = jnp.where(flags > 0, seq_ids[None, :] * windows + windows - 1, -1).reshape(-1)
    return (gene_slot.astype(jnp.int32), straddle.astype(jnp.int32))


def draw_gene_slot(key, part):
    return gene_layout(key)[0]


def draw_straddle_map(key, part):
    return gene_layout(key)[1]


def levels(stream_key, extent, cuts, least, high):
    def one(axis_at, blocks):
        steps = jax.random.uniform(jax.random.fold_in(jax.random.fold_in(stream_key, 6), axis_at), (blocks,), jnp.float32, least / len(cuts), high / len(cuts))
        return jnp.repeat(jnp.exp(steps), extent[axis_at] // blocks).reshape((-1,) + (1,) * (len(extent) - axis_at - 1))

    level = one(*cuts[0])
    for cut in cuts[1:]:
        level = level * one(*cut)
    return level


def normal_values(key, extent, deviation, most, shards=(), held_as=jnp.bfloat16):
    level = levels(key, extent, shards, -0.22, 0.18) if shards else 1.0
    values = jax.random.normal(key, extent, jnp.float32) * deviation * level
    return jnp.minimum(jnp.maximum(values, -most), most).astype(held_as)


def setup_inputs(seed: int = 0) -> dict:
    splits = jax.random.split(jax.random.key(seed), 9)
    return {
        "activations": normal_values(splits[0], (SEQS, LEN, C), 1.0, 6.0, ((1, 32), (2, 16))),
        "norm_gain": jnp.clip(1.0 + 0.18 * jax.random.normal(splits[1], (C,), jnp.float32), 0.1, 1.9),
        "norm_bias": jnp.clip(jax.random.uniform(splits[2], (C,), jnp.float32, -1.0, 1.0) * levels(splits[2], (C,), ((0, 16),), -0.4, 0.0), -1.0, 1.0),
        "conv_weight": normal_values(splits[3], (3, C, C), (3 * C) ** -0.5, 0.09375, ((2, 16),)),
        "head_weight": normal_values(splits[4], (C, TRACKS), C ** -0.5, 0.15625, ((1, 16),)),
        "head_bias": jnp.clip(-2.0 + 2.0 * jax.random.uniform(splits[5], (TRACKS,), jnp.float32) ** levels(splits[5], (TRACKS,), ((0, 16),), -0.2, 0.2), -2.0, 0.0),
        "gene_slot": draw_gene_slot(jax.random.fold_in(splits[8], 71), 0),
        "straddle_map": draw_straddle_map(jax.random.fold_in(splits[8], 71), 0),
    }


def reference(activations, norm_gain, norm_bias, conv_weight, head_weight, head_bias, gene_slot, straddle_map):
    def one_sequence(values):
        hidden = jax.nn.gelu(values.astype(jnp.float32) * norm_gain + norm_bias, approximate=True).astype(jnp.bfloat16)
        padded = jnp.pad(hidden, ((1, 1), (0, 0)))
        conv_out = jnp.zeros((LEN, C), jnp.float32)
        for offset in range(3):
            conv_out = conv_out + jnp.dot(padded[offset:offset + LEN], conv_weight[offset], preferred_element_type=jnp.float32)
        mixed = (values.astype(jnp.float32) + conv_out).astype(jnp.bfloat16)
        logits = jnp.dot(mixed, head_weight, preferred_element_type=jnp.float32)
        return jax.nn.softplus(logits + head_bias).astype(jnp.bfloat16)

    tracks = lax.map(one_sequence, activations)
    positions = jnp.arange(LEN, dtype=jnp.int32)
    block = (positions // POS_DEV).astype(jnp.int32)
    block = jnp.broadcast_to(block[None, :], gene_slot.shape)
    own_gene = block * GENES_DEV + gene_slot
    owner = jnp.maximum(block - 1, 0)
    entry = (owner * STRAD + jnp.clip(gene_slot - GENES_DEV, 0, STRAD - 1)).astype(jnp.int32)
    other_gene = owner * GENES_DEV + straddle_map[entry]
    gene_ids = jnp.where(gene_slot < 0, GENES, jnp.where(gene_slot < GENES_DEV, own_gene, other_gene)).astype(jnp.int32)
    flat_ids = gene_ids.reshape(-1)
    flat_tracks = tracks.reshape(-1, TRACKS).astype(jnp.float32)
    gene_sum = jax.ops.segment_sum(flat_tracks, flat_ids, num_segments=GENES + 1)[:GENES]
    gene_count = jax.ops.segment_sum(jnp.ones(flat_ids.shape, jnp.float32), flat_ids, num_segments=GENES + 1)[:GENES]
    gene_mean = gene_sum / jnp.maximum(gene_count, 1.0)[:, None]
    return tracks, gene_mean
```

```python
import functools

import jax
import jax.numpy as jnp
from jax import lax
from jax.experimental import pallas as pl
from jax.experimental.pallas import tpu as pltpu
from jax.sharding import PartitionSpec as P

MESH = pl.DeviceIdType.MESH
GENES_DEV = 32
STRAD = 4
SIDE = 4
BLK = 128


def kernel(
    n_pos, act, gain, bias, cw, hw, hb, gs, sm,
    tracks, gene_mean,
    raw, small, hid, cwb, hwb, prod, edge_out, edge_in, mix, out, acc, sums_in, strad_in, cnt_own, cnt_out, cnt_in, slots,
    send, recv, local,
):
    _, ch, length = act.shape
    group = SIDE * ch
    width = hb.shape[1]
    half = length // 2
    p = lax.axis_index("pos")
    t = lax.axis_index("trk")
    y, x = t // SIDE, t % SIDE

    def wrap(v, n):
        return lax.rem(v + n, n)

    def at_y(d):
        return wrap(y + d, SIDE)

    def at_x(d):
        return wrap(x + d, SIDE)

    def dev(dp=0, dy=0, dx=0):
        return (wrap(p + dp, n_pos), at_y(dy) * SIDE + at_x(dx))

    sibling = (p + 1 - 2 * lax.rem(p, 2), t)
    q = lax.rem(p, 4)
    q_z = lax.rem(q + 2, 4)
    q_s = q + 1 - 2 * lax.rem(q, 2)
    q_sz = lax.rem(q_s + 2, 4)

    used = [0, 0]
    started = []

    def remote(src, dst, device, landing):
        i = used[0]
        used[0] += 1
        copy = pltpu.make_async_remote_copy(
            src_ref=src, dst_ref=dst, send_sem=send.at[i], recv_sem=recv.at[i], device_id=device, device_id_type=MESH
        )
        copy.start()
        started.append(copy)
        return pltpu.make_async_remote_copy(
            src_ref=src, dst_ref=landing, send_sem=send.at[i], recv_sem=recv.at[i], device_id=device, device_id_type=MESH
        ).wait_recv

    def near(src, dst):
        i = used[1]
        used[1] += 1
        copy = pltpu.make_async_copy(src, dst, local.at[i])
        copy.start()
        return copy.wait

    partners = [dev(dy=d) for d in (1, 2, 3)] + [dev(dx=d) for d in (1, 2, 3)] + [dev(dp=d) for d in (1, -1, 2, -2)]
    partners += [dev(dp=s, dy=d) for s in (1, -1) for d in (1, 2, 3)]
    barrier = pltpu.get_barrier_semaphore()
    for partner in partners:
        pl.semaphore_signal(barrier, inc=1, device_id=partner, device_id_type=MESH)

    wait_own = [near(act.at[y, :, pl.ds(c * half, half)], raw.at[y, :, pl.ds(c * half, half)]) for c in range(2)]
    wait_cw = near(cw, cwb.at[:, y])
    wait_hw = [near(hw.at[:, k], hwb.at[y, k]) for k in range(SIDE)]
    small[y, :, :] = jnp.zeros(small.shape[1:], jnp.float32)
    small[y, 0:1, 0:ch] = gain[...]
    small[y, 1:2, 0:ch] = bias[...]
    small[y, 2:3, 0:width] = hb[...]
    rows = acc.shape[1]
    gene_ids = lax.broadcasted_iota(jnp.int32, (rows, length), 0)
    count = jnp.zeros((rows, 1), jnp.float32)
    for s in range(SIDE):
        count += jnp.sum((gs[s : s + 1, :] == gene_ids).astype(jnp.float32), axis=1, keepdims=True)
    count = jnp.broadcast_to(count, (rows, BLK))
    cnt_own[...] = count[:GENES_DEV]
    cnt_out[...] = count[GENES_DEV:]
    slots[...] = jnp.broadcast_to(gs[pl.ds(y, 1), :], slots.shape)
    pl.semaphore_wait(barrier, len(partners))

    wait_small = [remote(small.at[y], small.at[y], dev(dy=d), small.at[at_y(-d)]) for d in (1, 2, 3)]
    wait_raw = []
    for c in range(2):
        cols = pl.ds(c * half, half)
        wait_raw.append(
            [remote(act.at[at_y(d), :, cols], raw.at[y, :, cols], dev(dy=d), raw.at[at_y(-d), :, cols]) for d in (1, 2, 3)]
        )
    wait_cnt = remote(cnt_out, cnt_in, dev(dp=-1), cnt_in)

    def lanes(k):
        return pl.ds(pl.multiple_of(k * group, BLK), group)

    wait_cw1 = [
        remote(cw.at[:, :, lanes(q)], cwb.at[:, y, :, lanes(q)], dev(dy=d), cwb.at[:, at_y(-d), :, lanes(q)])
        for d in (1, 2, 3)
    ]

    wait_hid = []
    for w in wait_small:
        w()
    for c in range(2):
        cols = pl.ds(c * half, half)
        wait_own[c]()
        for w in wait_raw[c]:
            w()

        def activate(k, carry, cols=cols):
            vectors = jnp.transpose(small[k, :, 0:BLK])[0:ch]
            values = raw[k, :, cols].astype(jnp.float32) * vectors[:, 0:1] + vectors[:, 1:2]
            hid[k, x, :, cols] = jax.nn.gelu(values, approximate=True).astype(jnp.bfloat16)
            return carry

        lax.fori_loop(0, SIDE, activate, 0)
        wait_hid.append(
            [remote(hid.at[:, x, :, cols], hid.at[:, x, :, cols], dev(dx=d), hid.at[:, at_x(-d), :, cols]) for d in (1, 2, 3)]
        )

    low, high = pl.ds(0, ch // 2), pl.ds(ch // 2, ch // 2)
    wait_cw2, wait_cwz = [], []
    for d in (1, 2, 3):
        wait_cw1[d - 1]()
        k = at_y(-d)
        block = cwb.at[:, k, :, lanes(q)]
        wait_cwz.append(
            [
                remote(cwb.at[:, k, low, lanes(q)], cwb.at[:, k, low, lanes(q)], dev(dp=2), cwb.at[:, k, low, lanes(q_z)]),
                remote(cwb.at[:, k, high, lanes(q)], cwb.at[:, k, high, lanes(q)], dev(dp=-2), cwb.at[:, k, high, lanes(q_z)]),
            ]
        )
        wait_cw2.append(remote(block, block, sibling, cwb.at[:, k, :, lanes(q_s)]))
    wait_hw1 = [remote(hw.at[:, q], hwb.at[y, q], dev(dy=d), hwb.at[at_y(-d), q]) for d in (1, 2, 3)]
    for d in (1, 2, 3):
        k = at_y(-d)
        for w, part in zip(wait_cwz[d - 1], (low, high)):
            w()
            block = cwb.at[:, k, part, lanes(q_z)]
            wait_cw2.append(remote(block, block, sibling, cwb.at[:, k, part, lanes(q_sz)]))
    for w in wait_cw2:
        w()
    wait_cw()

    def products(c):
        cols = pl.ds(c * half, half)

        def tap(k, carry):
            prod[k, :, cols] = jnp.dot(
                cwb[k].reshape(group, SIDE * group),
                hid[:, :, :, cols].reshape(SIDE * group, half),
                preferred_element_type=jnp.float32,
            )
            return carry

        lax.fori_loop(0, 3, tap, 0)

    for w in wait_hid[0]:
        w()
    products(0)
    edge_out[1] = jnp.transpose(prod[2, :, 0:BLK])[0:8]
    wait_right = remote(edge_out.at[1], edge_in.at[1], dev(dp=-1), edge_in.at[1])

    first, last = pl.ds(0, SIDE // 2), pl.ds(SIDE // 2, SIDE // 2)
    wait_hw2, wait_hwz = [], []
    for d in (1, 2, 3):
        wait_hw1[d - 1]()
        k = at_y(-d)
        wait_hwz.append(
            [
                remote(hwb.at[k, q, first], hwb.at[k, q, first], dev(dp=2), hwb.at[k, q_z, first]),
                remote(hwb.at[k, q, last], hwb.at[k, q, last], dev(dp=-2), hwb.at[k, q_z, last]),
            ]
        )
        wait_hw2.append(remote(hwb.at[k, q], hwb.at[k, q], sibling, hwb.at[k, q_s]))

    for w in wait_hid[1]:
        w()
    products(1)
    edge_out[0] = jnp.transpose(prod[0, :, length - BLK : length])[BLK - 8 : BLK]
    wait_left = remote(edge_out.at[0], edge_in.at[0], dev(dp=1), edge_in.at[0])

    wait_mix = []
    lane = lax.broadcasted_iota(jnp.int32, (group, BLK), 1)
    row = lax.broadcasted_iota(jnp.int32, (BLK, group), 0)
    blocks = length // BLK
    order = list(range(1, blocks)) + [0]
    for b in order:
        here = slice(b * BLK, (b + 1) * BLK)
        before = pltpu.roll(prod[0, :, here], 1, 1)
        if b > 0:
            other = pltpu.roll(prod[0, :, (b - 1) * BLK : b * BLK], 1, 1)
        else:
            other = jnp.zeros_like(before)
        total = prod[1, :, here] + jnp.where(lane == 0, other, before)
        after = pltpu.roll(prod[2, :, here], BLK - 1, 1)
        if b < blocks - 1:
            other = pltpu.roll(prod[2, :, (b + 1) * BLK : (b + 2) * BLK], BLK - 1, 1)
        else:
            other = jnp.zeros_like(after)
        total += jnp.where(lane == BLK - 1, other, after)
        total += raw[:, :, here].reshape(group, BLK).astype(jnp.float32)
        total = jnp.transpose(total)
        if b == 0:
            wait_left()
            total += jnp.where((row == 0) & (p > 0), edge_in[0, 7:8, :], 0.0)
        if b == blocks - 1:
            wait_right()
            total += jnp.where((row == BLK - 1) & (p < n_pos - 1), edge_in[1, 0:1, :], 0.0)
        mix[here, lanes(x)] = total.astype(jnp.bfloat16)
        block = mix.at[pl.ds(b * BLK, BLK), lanes(x)]
        wait_mix.append(
            [remote(block, block, dev(dx=d), mix.at[pl.ds(b * BLK, BLK), lanes(at_x(-d))]) for d in (1, 2, 3)]
        )

    for d in (1, 2, 3):
        k = at_y(-d)
        for w, part in zip(wait_hwz[d - 1], (first, last)):
            w()
            wait_hw2.append(remote(hwb.at[k, q_z, part], hwb.at[k, q_z, part], sibling, hwb.at[k, q_sz, part]))
    for w in wait_hw2 + wait_hw:
        w()

    acc[...] = jnp.zeros_like(acc)
    wait_out = []
    for b, waits in zip(order, wait_mix):
        here = slice(b * BLK, (b + 1) * BLK)
        for w in waits:
            w()
        onehot = (slots[0:1, here] == lax.broadcasted_iota(jnp.int32, (rows, BLK), 0)).astype(jnp.bfloat16)
        for d in (1, 2, 3, 0):
            k = at_y(d)
            logits = jnp.dot(
                mix[here, :], hwb[k].reshape(SIDE * group, width), preferred_element_type=jnp.float32
            )
            logits += small[k, 2:3, 0:width]
            values = (jnp.maximum(logits, 0.0) + jnp.log1p(jnp.exp(-jnp.abs(logits)))).astype(jnp.bfloat16)
            out[d, here, :] = values
            acc[d] += jnp.dot(onehot, values, preferred_element_type=jnp.float32)
            spot = pl.ds(b * BLK, BLK)
            if d:
                wait_out.append(
                    remote(out.at[d, spot], tracks.at[y, spot], dev(dy=d), tracks.at[at_y(-d), spot])
                )
            else:
                wait_out.append(near(out.at[0, spot], tracks.at[y, spot]))

    own, tail = pl.ds(0, GENES_DEV), pl.ds(GENES_DEV, rows - GENES_DEV)
    wait_sums = [
        remote(acc.at[d, tail], strad_in.at[y], dev(dp=-1, dy=d), strad_in.at[at_y(-d)]) for d in range(SIDE)
    ]
    wait_sums += [remote(acc.at[d, own], sums_in.at[y], dev(dy=d), sums_in.at[at_y(-d)]) for d in (1, 2, 3)]
    wait_cnt()
    for w in wait_sums:
        w()
    totals = acc[0, 0:GENES_DEV, :]
    for d in (1, 2, 3):
        totals += sums_in[at_y(-d)]
    strays = strad_in[0] + strad_in[1] + strad_in[2] + strad_in[3]
    counts = cnt_own[...]
    gene = lax.broadcasted_iota(jnp.int32, (GENES_DEV, width), 0)
    for s in range(STRAD):
        totals += jnp.where(gene == sm[s], strays[s : s + 1, :], 0.0)
        counts += jnp.where(gene[:, 0:BLK] == sm[s], cnt_in[s : s + 1, :], 0.0)
    gene_mean[...] = totals / jnp.maximum(counts, 1.0)[:, 0:1]
    for w in wait_out:
        w()
    for copy in started:
        copy.wait_send()


def solution(mesh):
    n_pos = mesh.shape["pos"]

    def per_device(act, gain, bias, cw, hw, hb, gs, sm):
        seqs, length, ch = act.shape
        group = SIDE * ch
        width = hw.shape[1]
        rows = GENES_DEV + 8
        f32, bf16 = jnp.float32, jnp.bfloat16
        anywhere = pl.BlockSpec(memory_space=pl.ANY)
        vmem = pl.BlockSpec(memory_space=pltpu.VMEM)
        tracks, gene_mean = pl.pallas_call(
            functools.partial(kernel, n_pos),
            name="fused_block",
            out_shape=(
                jax.ShapeDtypeStruct((seqs, length, width), bf16),
                jax.ShapeDtypeStruct((GENES_DEV, width), f32),
            ),
            in_specs=[
                anywhere, vmem, vmem, anywhere, anywhere, vmem, vmem,
                pl.BlockSpec(memory_space=pltpu.SMEM),
            ],
            out_specs=(anywhere, vmem),
            scratch_shapes=[
                pltpu.VMEM((SIDE, ch, length), bf16),
                pltpu.VMEM((SIDE, 8, 256), f32),
                pltpu.VMEM((SIDE, SIDE, ch, length), bf16),
                pltpu.VMEM((3, SIDE, ch, SIDE * group), bf16),
                pltpu.VMEM((SIDE, SIDE, SIDE, ch, width), bf16),
                pltpu.VMEM((3, group, length), f32),
                pltpu.VMEM((2, 8, group), f32),
                pltpu.VMEM((2, 8, group), f32),
                pltpu.VMEM((length, SIDE * group), bf16),
                pltpu.VMEM((SIDE, length, width), bf16),
                pltpu.VMEM((SIDE, rows, width), f32),
                pltpu.VMEM((SIDE, GENES_DEV, width), f32),
                pltpu.VMEM((SIDE, 8, width), f32),
                pltpu.VMEM((GENES_DEV, BLK), f32),
                pltpu.VMEM((8, BLK), f32),
                pltpu.VMEM((8, BLK), f32),
                pltpu.VMEM((8, length), jnp.int32),
                pltpu.SemaphoreType.DMA((96,)),
                pltpu.SemaphoreType.DMA((96,)),
                pltpu.SemaphoreType.DMA((16,)),
            ],
            compiler_params=pltpu.CompilerParams(
                collective_id=0, has_side_effects=True, vmem_limit_bytes=48 * 2**20
            ),
        )(
            jnp.transpose(act, (0, 2, 1)),
            gain.reshape(1, ch),
            bias.reshape(1, ch),
            jnp.transpose(cw, (0, 2, 1)),
            hw.reshape(SIDE, SIDE, ch, width),
            hb.reshape(1, width),
            gs,
            sm,
        )
        return tracks, gene_mean

    in_specs = (
        P(None, "pos", "trk"),
        P("trk"),
        P("trk"),
        P(None, None, "trk"),
        P(None, "trk"),
        P("trk"),
        P(None, "pos"),
        P("pos"),
    )
    out_specs = (P(None, "pos", "trk"), P("pos", "trk"))
    return jax.shard_map(per_device, mesh=mesh, in_specs=in_specs, out_specs=out_specs, check_vma=False)
```

```python
import functools

import jax
import jax.numpy as jnp
from jax import lax
from jax.experimental import pallas as pl
from jax.experimental.pallas import tpu as pltpu
from jax.sharding import PartitionSpec as P

MESH = pl.DeviceIdType.MESH
GENES_DEV = 32
STRAD = 4
SIDE = 4
BLK = 128


def kernel(
    n_pos, act, gain, bias, cw, hw, hb, gs, sm,
    tracks, gene_mean,
    gain_v, bias_v, hb_v, gs_v, sm_v, raw, small, hid, cwb, hwb, prod, edge_out, edge_in, mix, out, acc, sums_in, strad_in, cnt_own, cnt_out, cnt_in, slots,
    send, recv, local,
):
    _, ch, length = act.shape
    group = SIDE * ch
    width = hb.shape[1]
    half = length // 2
    p = lax.axis_index("pos")
    t = lax.axis_index("trk")
    y, x = t // SIDE, t % SIDE

    def wrap(v, n):
        return lax.rem(v + n, n)

    def at_y(d):
        return wrap(y + d, SIDE)

    def at_x(d):
        return wrap(x + d, SIDE)

    def dev(dp=0, dy=0, dx=0):
        return (wrap(p + dp, n_pos), at_y(dy) * SIDE + at_x(dx))

    sibling = (p + 1 - 2 * lax.rem(p, 2), t)
    q = lax.rem(p, 4)
    q_z = lax.rem(q + 2, 4)
    q_s = q + 1 - 2 * lax.rem(q, 2)
    q_sz = lax.rem(q_s + 2, 4)

    used = [0, 0]
    started = []

    pending = []

    def once(wait):
        done = []

        def call():
            if not done:
                done.append(True)
                wait()

        pending.append(call)
        return call

    def finish():
        for w in pending:
            w()
        for copy in started:
            copy.wait_send()

    def remote(src, dst, device, landing):
        i = used[0]
        used[0] += 1
        copy = pltpu.make_async_remote_copy(
            src_ref=src, dst_ref=dst, send_sem=send.at[i], recv_sem=recv.at[i], device_id=device, device_id_type=MESH
        )
        copy.start()
        started.append(copy)
        arrival = pltpu.make_async_remote_copy(
            src_ref=src, dst_ref=landing, send_sem=send.at[i], recv_sem=recv.at[i], device_id=device, device_id_type=MESH
        )
        return once(arrival.wait_recv)

    def near(src, dst):
        i = used[1]
        used[1] += 1
        copy = pltpu.make_async_copy(src, dst, local.at[i])
        copy.start()
        return once(copy.wait)

    partners = [dev(dy=d) for d in (1, 2, 3)] + [dev(dx=d) for d in (1, 2, 3)] + [dev(dp=d) for d in (1, -1, 2, -2)]
    partners += [dev(dp=s, dy=d) for s in (1, -1) for d in (1, 2, 3)]
    barrier = pltpu.get_barrier_semaphore()
    for partner in partners:
        pl.semaphore_signal(barrier, inc=1, device_id=partner, device_id_type=MESH)

    wait_own = [near(act.at[y, :, pl.ds(c * half, half)], raw.at[y, :, pl.ds(c * half, half)]) for c in range(2)]
    wait_vectors = [near(*pair) for pair in ((gain, gain_v), (bias, bias_v), (hb, hb_v), (gs, gs_v), (sm, sm_v))]
    wait_cw = near(cw, cwb.at[:, y])
    wait_hw = [near(hw.at[:, k], hwb.at[y, k]) for k in range(SIDE)]
    small[y, :, :] = jnp.zeros(small.shape[1:], jnp.float32)
    for w in wait_vectors:
        w()
    small[y, 0:1, 0:ch] = gain_v[...]
    small[y, 1:2, 0:ch] = bias_v[...]
    small[y, 2:3, 0:width] = hb_v[...]
    pl.semaphore_wait(barrier, len(partners))

    wait_small = [remote(small.at[y], small.at[y], dev(dy=d), small.at[at_y(-d)]) for d in (1, 2, 3)]

    def raw_to_column(c):
        cols = pl.ds(c * half, half)
        return [
            remote(act.at[at_y(d), :, cols], raw.at[y, :, cols], dev(dy=d), raw.at[at_y(-d), :, cols]) for d in (1, 2, 3)
        ]

    def ring_first(view, spots, up, down):
        mine = view(spots[0], None)
        return remote(mine, mine, up, view(spots[1], None)), remote(mine, mine, down, view(spots[2], None))

    def ring_second(view, spots, up, down, waits):
        waits[0]()
        block = view(spots[1], 0)
        low = remote(block, block, up, view(spots[3], 0))
        waits[1]()
        block = view(spots[2], 1)
        high = remote(block, block, down, view(spots[3], 1))
        return low, high

    spots_y = (y, at_y(-1), at_y(1), at_y(2))
    spots_x = (x, at_x(-1), at_x(1), at_x(2))
    up_y, down_y, up_x, down_x = dev(dy=1), dev(dy=-1), dev(dx=1), dev(dx=-1)
    above, below = dev(dp=2), dev(dp=-2)

    def lanes(k):
        return pl.ds(pl.multiple_of(k * group, BLK), group)

    def cw_view(tap):
        def of(quarter):
            def view(k, part):
                if part is None:
                    return cwb.at[tap, k, :, lanes(quarter)]
                return cwb.at[tap, k, pl.ds(part * (ch // 2), ch // 2), lanes(quarter)]

            return view

        return of

    def hw_view(quarter):
        def view(k, part):
            if part is None:
                return hwb.at[k, quarter]
            return hwb.at[k, quarter, pl.ds(part * (SIDE // 2), SIDE // 2)]

        return view

    def to_z(view, k):
        return [
            remote(view(q)(k, 0), view(q)(k, 0), above, view(q_z)(k, 0)),
            remote(view(q)(k, 1), view(q)(k, 1), below, view(q_z)(k, 1)),
        ]

    def to_sibling(view, k, part, mine, theirs):
        return remote(view(mine)(k, part), view(mine)(k, part), sibling, view(theirs)(k, part))

    def weights_second(view, ring):
        opposite = ring_second(view(q), spots_y, up_y, down_y, ring)
        from_z, from_sibling = [], []
        for k in spots_y[1:3]:
            from_z += to_z(view, k)
            from_sibling.append(to_sibling(view, k, None, q, q_s))
        return opposite, from_z, from_sibling

    def weights_third(view, opposite, from_z, from_sibling):
        for w in opposite:
            w()
        from_z += to_z(view, spots_y[3])
        from_sibling.append(to_sibling(view, spots_y[3], None, q, q_s))

    def weights_fourth(view, from_z, from_sibling, which):
        for i in which:
            from_z[2 * i]()
            from_z[2 * i + 1]()
            from_sibling.append(to_sibling(view, spots_y[1 + i], None, q_z, q_sz))

    def hid_view(c):
        def view(k, part):
            if part is None:
                return hid.at[:, k, :, pl.ds(c * half, half)]
            return hid.at[pl.ds(part * (SIDE // 2), SIDE // 2), k, :, pl.ds(c * half, half)]

        return view

    def activate(c):
        cols = pl.ds(c * half, half)
        wait_own[c]()
        for w in wait_raw[c]:
            w()

        def channels(k, carry):
            vectors = jnp.transpose(small[k, :, 0:BLK])[0:ch]
            values = raw[k, :, cols].astype(jnp.float32) * vectors[:, 0:1] + vectors[:, 1:2]
            hid[k, x, :, cols] = jax.nn.gelu(values, approximate=True).astype(jnp.bfloat16)
            return carry

        lax.fori_loop(0, SIDE, channels, 0)
        return ring_first(hid_view(c), spots_x, up_x, down_x)

    taps = range(3)
    cw_of = [cw_view(tap) for tap in taps]
    wait_raw = [raw_to_column(0)]
    wait_cw()
    cw_ring = [ring_first(cw_of[0](q), spots_y, up_y, down_y)]
    wait_raw.append(raw_to_column(1))
    for tap in (1, 2):
        cw_ring.append(ring_first(cw_of[tap](q), spots_y, up_y, down_y))

    rows = acc.shape[1]
    gene_ids = lax.broadcasted_iota(jnp.int32, (rows, length), 0)
    count = jnp.zeros((rows, 1), jnp.float32)
    for s in range(SIDE):
        count += jnp.sum((gs_v[s : s + 1, :] == gene_ids).astype(jnp.float32), axis=1, keepdims=True)
    count = jnp.broadcast_to(count, (rows, BLK))
    cnt_own[...] = count[:GENES_DEV]
    cnt_out[...] = count[GENES_DEV:]
    slots[...] = jnp.broadcast_to(gs_v[pl.ds(y, 1), :], slots.shape)
    wait_cnt = remote(cnt_out, cnt_in, dev(dp=-1), cnt_in)

    for w in wait_small:
        w()
    hid_ring = [activate(0)]
    cw_parts = [weights_second(cw_of[0], cw_ring[0])]
    hid_ring.append(activate(1))
    cw_parts.append(weights_second(cw_of[1], cw_ring[1]))
    cw_parts.append(weights_second(cw_of[2], cw_ring[2]))
    for w in wait_hw:
        w()
    hw_ring = ring_first(hw_view(q), spots_y, up_y, down_y)
    weights_fourth(cw_of[0], *cw_parts[0][1:], (0, 1))
    weights_third(cw_of[0], *cw_parts[0])
    hid_far = [ring_second(hid_view(0), spots_x, up_x, down_x, hid_ring[0])]
    weights_third(cw_of[1], *cw_parts[1])
    weights_third(cw_of[2], *cw_parts[2])
    weights_fourth(cw_of[1], *cw_parts[1][1:], (0, 1))
    weights_fourth(cw_of[2], *cw_parts[2][1:], (0, 1))
    weights_fourth(cw_of[0], *cw_parts[0][1:], (2,))
    hid_far.append(ring_second(hid_view(1), spots_x, up_x, down_x, hid_ring[1]))
    weights_fourth(cw_of[1], *cw_parts[1][1:], (2,))
    weights_fourth(cw_of[2], *cw_parts[2][1:], (2,))

    def product(tap, c):
        cols = pl.ds(c * half, half)
        for w in (*cw_parts[tap][2], *hid_far[c]):
            w()
        prod[tap, :, cols] = jnp.dot(
            cwb[tap].reshape(group, SIDE * group),
            hid[:, :, :, cols].reshape(SIDE * group, half),
            preferred_element_type=jnp.float32,
        )

    product(0, 0)
    product(1, 0)
    hw_parts = weights_second(hw_view, hw_ring)
    product(2, 0)
    edge_out[1] = jnp.transpose(prod[2, :, 0:BLK])[0:8]
    wait_right = remote(edge_out.at[1], edge_in.at[1], dev(dp=-1), edge_in.at[1])
    product(2, 1)

    def mix_view(first, size):
        def view(k, part):
            if part is None:
                return mix.at[pl.ds(first, size), lanes(k)]
            return mix.at[pl.ds(first + part * (size // 2), size // 2), lanes(k)]

        return view

    lane = lax.broadcasted_iota(jnp.int32, (group, BLK), 1)
    row = lax.broadcasted_iota(jnp.int32, (BLK, group), 0)
    blocks = length // BLK
    pieces = [(b * BLK, BLK) for b in range(1, blocks)] + [(0, BLK // 2), (BLK // 2, BLK // 2)]

    def mixed(b):
        here = slice(b * BLK, (b + 1) * BLK)
        before = pltpu.roll(prod[0, :, here], 1, 1)
        if b > 0:
            other = pltpu.roll(prod[0, :, (b - 1) * BLK : b * BLK], 1, 1)
        else:
            other = jnp.zeros_like(before)
        total = prod[1, :, here] + jnp.where(lane == 0, other, before)
        after = pltpu.roll(prod[2, :, here], BLK - 1, 1)
        if b < blocks - 1:
            other = pltpu.roll(prod[2, :, (b + 1) * BLK : (b + 2) * BLK], BLK - 1, 1)
        else:
            other = jnp.zeros_like(after)
        total += jnp.where(lane == BLK - 1, other, after)
        total += raw[:, :, here].reshape(group, BLK).astype(jnp.float32)
        total = jnp.transpose(total)
        if b == 0:
            wait_left()
            total += jnp.where((row == 0) & (p > 0), edge_in[0, 7:8, :], 0.0)
        if b == blocks - 1:
            wait_right()
            total += jnp.where((row == BLK - 1) & (p < n_pos - 1), edge_in[1, 0:1, :], 0.0)
        mix[here, lanes(x)] = total.astype(jnp.bfloat16)

    own, tail = pl.ds(0, GENES_DEV), pl.ds(GENES_DEV, rows - GENES_DEV)
    wait_sums = []

    def head(first, size, final):
        here = slice(first, first + size)
        spot = pl.ds(first, size)
        onehot = (slots[0:1, here] == lax.broadcasted_iota(jnp.int32, (rows, size), 0)).astype(jnp.bfloat16)
        for d in (2, 1, 3, 0):
            k = at_y(d)
            logits = jnp.dot(
                mix[here, :], hwb[k].reshape(SIDE * group, width), preferred_element_type=jnp.float32
            )
            logits += small[k, 2:3, 0:width]
            values = (jnp.maximum(logits, 0.0) + jnp.log1p(jnp.exp(-jnp.abs(logits)))).astype(jnp.bfloat16)
            out[d, here, :] = values
            acc[d] += jnp.dot(onehot, values, preferred_element_type=jnp.float32)
            if final:
                wait_sums.append(remote(acc.at[d, tail], strad_in.at[y], dev(dp=-1, dy=d), strad_in.at[at_y(-d)]))
                if d:
                    wait_sums.append(remote(acc.at[d, own], sums_in.at[y], dev(dy=d), sums_in.at[at_y(-d)]))
            if d:
                remote(out.at[d, spot], tracks.at[y, spot], dev(dy=d), tracks.at[at_y(-d), spot])
            else:
                near(out.at[0, spot], tracks.at[y, spot])

    mix_ring, mix_far = [], []

    def mix_first(i):
        mix_ring.append(ring_first(mix_view(*pieces[i]), spots_x, up_x, down_x))

    def mix_second(i):
        mix_far.append(ring_second(mix_view(*pieces[i]), spots_x, up_x, down_x, mix_ring[i]))

    mixed(1)
    mix_first(0)
    acc[...] = jnp.zeros_like(acc)
    product(0, 1)
    edge_out[0] = jnp.transpose(prod[0, :, length - BLK : length])[BLK - 8 : BLK]
    wait_left = remote(edge_out.at[0], edge_in.at[0], dev(dp=1), edge_in.at[0])
    product(1, 1)
    mixed(2)
    mix_first(1)
    weights_third(hw_view, *hw_parts)
    mixed(3)
    mix_second(0)
    mix_first(2)
    weights_fourth(hw_view, *hw_parts[1:], (0, 1))
    mixed(0)
    mix_second(1)
    mix_first(3)
    mix_first(4)
    weights_fourth(hw_view, *hw_parts[1:], (2,))
    for w in hw_parts[2]:
        w()
    for i, piece in enumerate(pieces):
        for w in mix_far[i]:
            w()
        head(*piece, i == len(pieces) - 1)
        if i + 2 < len(pieces):
            mix_second(i + 2)

    wait_cnt()
    for w in wait_sums:
        w()
    totals = acc[0, 0:GENES_DEV, :]
    for d in (1, 2, 3):
        totals += sums_in[at_y(-d)]
    strays = strad_in[0] + strad_in[1] + strad_in[2] + strad_in[3]
    counts = cnt_own[...]
    gene = lax.broadcasted_iota(jnp.int32, (GENES_DEV, width), 0)
    for s in range(STRAD):
        totals += jnp.where(gene == sm_v[0:1, s : s + 1], strays[s : s + 1, :], 0.0)
        counts += jnp.where(gene[:, 0:BLK] == sm_v[0:1, s : s + 1], cnt_in[s : s + 1, :], 0.0)
    gene_mean[...] = totals / jnp.maximum(counts, 1.0)[:, 0:1]
    finish()


def solution(mesh):
    n_pos = mesh.shape["pos"]

    def per_device(act, gain, bias, cw, hw, hb, gs, sm):
        seqs, length, ch = act.shape
        group = SIDE * ch
        width = hw.shape[1]
        rows = GENES_DEV + 8
        f32, bf16 = jnp.float32, jnp.bfloat16
        anywhere = pl.BlockSpec(memory_space=pl.ANY)
        hbm = pl.BlockSpec(memory_space=pltpu.HBM)
        vmem = pl.BlockSpec(memory_space=pltpu.VMEM)
        operands = (
            jnp.transpose(act, (0, 2, 1)),
            gain.reshape(1, ch),
            bias.reshape(1, ch),
            jnp.transpose(cw, (0, 2, 1)),
            hw.reshape(SIDE, SIDE, ch, width),
            hb.reshape(1, width),
            gs,
            sm.reshape(1, STRAD),
        )
        tracks, gene_mean = pl.pallas_call(
            functools.partial(kernel, n_pos),
            name="fused_block",
            out_shape=(
                pltpu.VMEM((seqs, length, width), bf16),
                jax.ShapeDtypeStruct((GENES_DEV, width), f32),
            ),
            in_specs=[hbm] * 8,
            out_specs=(anywhere, vmem),
            scratch_shapes=[
                pltpu.VMEM((1, ch), f32),
                pltpu.VMEM((1, ch), f32),
                pltpu.VMEM((1, width), f32),
                pltpu.VMEM((seqs, length), jnp.int32),
                pltpu.VMEM((1, STRAD), jnp.int32),
                pltpu.VMEM((SIDE, ch, length), bf16),
                pltpu.VMEM((SIDE, 8, 256), f32),
                pltpu.VMEM((SIDE, SIDE, ch, length), bf16),
                pltpu.VMEM((3, SIDE, ch, SIDE * group), bf16),
                pltpu.VMEM((SIDE, SIDE, SIDE, ch, width), bf16),
                pltpu.VMEM((3, group, length), f32),
                pltpu.VMEM((2, 8, group), f32),
                pltpu.VMEM((2, 8, group), f32),
                pltpu.VMEM((length, SIDE * group), bf16),
                pltpu.VMEM((SIDE, length, width), bf16),
                pltpu.VMEM((SIDE, rows, width), f32),
                pltpu.VMEM((SIDE, GENES_DEV, width), f32),
                pltpu.VMEM((SIDE, 8, width), f32),
                pltpu.VMEM((GENES_DEV, BLK), f32),
                pltpu.VMEM((8, BLK), f32),
                pltpu.VMEM((8, BLK), f32),
                pltpu.VMEM((8, length), jnp.int32),
                pltpu.SemaphoreType.DMA((160,)),
                pltpu.SemaphoreType.DMA((160,)),
                pltpu.SemaphoreType.DMA((24,)),
            ],
            compiler_params=pltpu.CompilerParams(
                collective_id=0, has_side_effects=True, vmem_limit_bytes=48 * 2**20
            ),
        )(*(pltpu.with_memory_space_constraint(operand, pltpu.HBM) for operand in operands))
        return tracks, gene_mean

    in_specs = (
        P(None, "pos", "trk"),
        P("trk"),
        P("trk"),
        P(None, None, "trk"),
        P(None, "trk"),
        P("trk"),
        P(None, "pos"),
        P("pos"),
    )
    out_specs = (P(None, "pos", "trk"), P("pos", "trk"))
    return jax.shard_map(per_device, mesh=mesh, in_specs=in_specs, out_specs=out_specs, check_vma=False)
```

```python
import functools

import jax
import jax.numpy as jnp
from jax import lax
from jax.experimental import pallas as pl
from jax.experimental.pallas import tpu as pltpu
from jax.sharding import PartitionSpec as P

MESH = pl.DeviceIdType.MESH
GENES_DEV = 32
STRAD = 4
SIDE = 4
BLK = 128


def kernel(
    n_pos, act, gain, bias, cw, hw, hb, gs, sm,
    tracks, gene_mean,
    gain_v, bias_v, hb_v, gs_v, sm_v, raw, small, hid, cwb, hwb, prod, edge_out, edge_in, mix, out, acc, sums_out, sums_in, strad_in, cnt_own, cnt_out, cnt_in, slots,
    send, recv, local,
):
    _, ch, length = act.shape
    group = SIDE * ch
    width = hb.shape[1]
    half = length // 2
    p = lax.axis_index("pos")
    t = lax.axis_index("trk")
    y, x = t // SIDE, t % SIDE

    def wrap(v, n):
        return lax.rem(v + n, n)

    def at_y(d):
        return wrap(y + d, SIDE)

    def at_x(d):
        return wrap(x + d, SIDE)

    def dev(dp=0, dy=0, dx=0):
        return (wrap(p + dp, n_pos), at_y(dy) * SIDE + at_x(dx))

    sibling = (p + 1 - 2 * lax.rem(p, 2), t)
    q = lax.rem(p, 4)
    q_z = lax.rem(q + 2, 4)
    q_s = q + 1 - 2 * lax.rem(q, 2)
    q_sz = lax.rem(q_s + 2, 4)

    used = [0, 0]
    started = []

    pending = []

    def once(wait):
        done = []

        def call():
            if not done:
                done.append(True)
                wait()

        pending.append(call)
        return call

    def finish():
        for w in pending:
            w()
        for copy in started[-19:]:
            copy.wait_send()

    def remote(src, dst, device, landing):
        i = used[0]
        used[0] += 1
        copy = pltpu.make_async_remote_copy(
            src_ref=src, dst_ref=dst, send_sem=send.at[i], recv_sem=recv.at[i], device_id=device, device_id_type=MESH
        )
        copy.start()
        started.append(copy)
        arrival = pltpu.make_async_remote_copy(
            src_ref=src, dst_ref=landing, send_sem=send.at[i], recv_sem=recv.at[i], device_id=device, device_id_type=MESH
        )
        return once(arrival.wait_recv)

    def near(src, dst):
        i = used[1]
        used[1] += 1
        copy = pltpu.make_async_copy(src, dst, local.at[i])
        copy.start()
        return once(copy.wait)

    wait_vectors = [near(*pair) for pair in ((gain, gain_v), (bias, bias_v), (hb, hb_v), (gs, gs_v), (sm, sm_v))]

    partners = [dev(dy=d) for d in (1, 2, 3)] + [dev(dx=d) for d in (1, 3)] + [dev(dp=d) for d in (1, -1, 2, -2)]
    partners += [dev(dp=s, dy=d) for s in (1, -1) for d in (1, 2, 3)]
    barrier = pltpu.get_barrier_semaphore()
    for partner in partners:
        pl.semaphore_signal(barrier, inc=1, device_id=partner, device_id_type=MESH)

    pl.semaphore_wait(barrier, len(partners))

    def raw_to_column(c, which):
        cols = pl.ds(c * half, half)
        return [
            remote(act.at[at_y(d), :, cols], raw.at[y, :, cols], dev(dy=d), raw.at[at_y(-d), :, cols]) for d in which
        ]

    wait_raw = [raw_to_column(0, (2,))]
    small[y, :, :] = jnp.zeros(small.shape[1:], jnp.float32)
    for w in wait_vectors:
        w()
    small[y, 0:1, 0:ch] = gain_v[...]
    small[y, 1:2, 0:ch] = bias_v[...]
    small[y, 2:3, 0:width] = hb_v[...]
    wait_small = [remote(small.at[y], small.at[y], dev(dy=d), small.at[at_y(-d)]) for d in (2, 1, 3)]
    wait_raw[0] += raw_to_column(0, (1, 3))

    def ring_first(view, spots, up, down, mine=None):
        here = view(spots[0], None)
        mine = here if mine is None else mine
        return remote(mine, here, up, view(spots[1], None)), remote(mine, here, down, view(spots[2], None))

    def ring_second(view, spots, up, down, waits):
        waits[0]()
        block = view(spots[1], 0)
        low = remote(block, block, up, view(spots[3], 0))
        waits[1]()
        block = view(spots[2], 1)
        high = remote(block, block, down, view(spots[3], 1))
        return low, high

    spots_y = (y, at_y(-1), at_y(1), at_y(2))
    spots_x = (x, at_x(-1), at_x(1), at_x(2))
    up_y, down_y, up_x, down_x = dev(dy=1), dev(dy=-1), dev(dx=1), dev(dx=-1)
    above, below = dev(dp=2), dev(dp=-2)

    def lanes(k):
        return pl.ds(pl.multiple_of(k * group, BLK), group)

    def cw_view(tap):
        def of(quarter):
            def view(k, part):
                if part is None:
                    return cwb.at[tap, k, :, lanes(quarter)]
                return cwb.at[tap, k, pl.ds(part * (ch // 2), ch // 2), lanes(quarter)]

            return view

        return of

    def hw_view(quarter):
        def view(k, part):
            if part is None:
                return hwb.at[k, quarter]
            return hwb.at[k, quarter, pl.ds(part * (SIDE // 2), SIDE // 2)]

        return view

    def to_z(view, k):
        return [
            remote(view(q)(k, 0), view(q)(k, 0), above, view(q_z)(k, 0)),
            remote(view(q)(k, 1), view(q)(k, 1), below, view(q_z)(k, 1)),
        ]

    def to_sibling(view, k, part, mine, theirs):
        return remote(view(mine)(k, part), view(mine)(k, part), sibling, view(theirs)(k, part))

    def weights_second(view, ring):
        opposite = ring_second(view(q), spots_y, up_y, down_y, ring)
        from_z, from_sibling = [], []
        for k in spots_y[1:3]:
            from_z += to_z(view, k)
            from_sibling.append(to_sibling(view, k, None, q, q_s))
        return opposite, from_z, from_sibling

    def weights_third(view, opposite, from_z, from_sibling):
        for w in opposite:
            w()
        from_z += to_z(view, spots_y[3])
        from_sibling.append(to_sibling(view, spots_y[3], None, q, q_s))

    def weights_fourth(view, from_z, from_sibling, which):
        for i in which:
            from_z[2 * i]()
            from_z[2 * i + 1]()
            from_sibling.append(to_sibling(view, spots_y[1 + i], None, q_z, q_sz))

    def hid_view(c):
        def view(k, part):
            if part is None:
                return hid.at[:, k, :, pl.ds(c * half, half)]
            return hid.at[pl.ds(part * (SIDE // 2), SIDE // 2), k, :, pl.ds(c * half, half)]

        return view

    def activate(c):
        cols = pl.ds(c * half, half)
        wait_own[c]()
        for w in wait_raw[c]:
            w()

        def channels(k, carry):
            vectors = jnp.transpose(small[k, :, 0:BLK])[0:ch]
            values = raw[k, :, cols].astype(jnp.float32) * vectors[:, 0:1] + vectors[:, 1:2]
            hid[k, x, :, cols] = jax.nn.gelu(values, approximate=True).astype(jnp.bfloat16)
            return carry

        lax.fori_loop(0, SIDE, channels, 0)
        return ring_first(hid_view(c), spots_x, up_x, down_x)

    taps = range(3)
    cw_of = [cw_view(tap) for tap in taps]

    def cw_first(tap):
        return ring_first(cw_of[tap](q), spots_y, up_y, down_y, cw.at[tap, :, lanes(q)])

    cw_ring = [cw_first(0)]
    wait_raw.append(raw_to_column(1, (2, 1, 3)))
    wait_own = [near(act.at[y, :, pl.ds(c * half, half)], raw.at[y, :, pl.ds(c * half, half)]) for c in range(2)]
    cw_ring += [cw_first(1), cw_first(2)]
    wait_cw = near(cw, cwb.at[:, y])
    wait_hw = [near(hw.at[:, k], hwb.at[y, k]) for k in range(SIDE)]

    rows = acc.shape[1]
    gene_ids = lax.broadcasted_iota(jnp.int32, (rows, length), 0)
    count = jnp.zeros((rows, 1), jnp.float32)
    for s in range(SIDE):
        count += jnp.sum((gs_v[s : s + 1, :] == gene_ids).astype(jnp.float32), axis=1, keepdims=True)
    count = jnp.broadcast_to(count, (rows, BLK))
    cnt_own[...] = count[:GENES_DEV]
    cnt_out[...] = count[GENES_DEV:]
    slots[...] = jnp.broadcast_to(gs_v[pl.ds(y, 1), :], slots.shape)
    wait_cnt = remote(cnt_out, cnt_in, dev(dp=-1), cnt_in)

    for w in wait_small:
        w()
    hid_ring = [activate(0)]
    cw_parts = [weights_second(cw_of[0], cw_ring[0])]
    hid_ring.append(activate(1))
    cw_parts.append(weights_second(cw_of[1], cw_ring[1]))
    cw_parts.append(weights_second(cw_of[2], cw_ring[2]))
    for w in wait_hw:
        w()
    hw_ring = ring_first(hw_view(q), spots_y, up_y, down_y)
    weights_fourth(cw_of[0], *cw_parts[0][1:], (0, 1))
    weights_third(cw_of[0], *cw_parts[0])
    hid_far = [ring_second(hid_view(0), spots_x, up_x, down_x, hid_ring[0])]
    weights_third(cw_of[1], *cw_parts[1])
    weights_third(cw_of[2], *cw_parts[2])
    weights_fourth(cw_of[1], *cw_parts[1][1:], (0, 1))
    weights_fourth(cw_of[2], *cw_parts[2][1:], (0, 1))
    weights_fourth(cw_of[0], *cw_parts[0][1:], (2,))
    hid_far.append(ring_second(hid_view(1), spots_x, up_x, down_x, hid_ring[1]))
    weights_fourth(cw_of[1], *cw_parts[1][1:], (2,))
    weights_fourth(cw_of[2], *cw_parts[2][1:], (2,))

    def product(tap, c):
        cols = pl.ds(c * half, half)
        wait_cw()
        for w in (*cw_parts[tap][2], *hid_far[c]):
            w()
        prod[tap, :, cols] = jnp.dot(
            cwb[tap].reshape(group, SIDE * group),
            hid[:, :, :, cols].reshape(SIDE * group, half),
            preferred_element_type=jnp.float32,
        )

    product(0, 0)
    product(1, 0)
    hw_parts = weights_second(hw_view, hw_ring)
    product(2, 0)
    edge_out[1] = jnp.transpose(prod[2, :, 0:BLK])[0:8]
    wait_right = remote(edge_out.at[1], edge_in.at[1], dev(dp=-1), edge_in.at[1])
    product(2, 1)

    def mix_view(first, size):
        def view(k, part):
            if part is None:
                return mix.at[pl.ds(first, size), lanes(k)]
            return mix.at[pl.ds(first + part * (size // 2), size // 2), lanes(k)]

        return view

    lane = lax.broadcasted_iota(jnp.int32, (group, BLK), 1)
    row = lax.broadcasted_iota(jnp.int32, (BLK, group), 0)
    blocks = length // BLK
    order = list(range(1, blocks)) + [0]
    pieces = [(b * BLK, BLK) for b in order]

    def mixed(b):
        here = slice(b * BLK, (b + 1) * BLK)
        before = pltpu.roll(prod[0, :, here], 1, 1)
        if b > 0:
            other = pltpu.roll(prod[0, :, (b - 1) * BLK : b * BLK], 1, 1)
        else:
            other = jnp.zeros_like(before)
        total = prod[1, :, here] + jnp.where(lane == 0, other, before)
        after = pltpu.roll(prod[2, :, here], BLK - 1, 1)
        if b < blocks - 1:
            other = pltpu.roll(prod[2, :, (b + 1) * BLK : (b + 2) * BLK], BLK - 1, 1)
        else:
            other = jnp.zeros_like(after)
        total += jnp.where(lane == BLK - 1, other, after)
        total += raw[:, :, here].reshape(group, BLK).astype(jnp.float32)
        total = jnp.transpose(total)
        if b == 0:
            wait_left()
            total += jnp.where((row == 0) & (p > 0), edge_in[0, 7:8, :], 0.0)
        if b == blocks - 1:
            wait_right()
            total += jnp.where((row == BLK - 1) & (p < n_pos - 1), edge_in[1, 0:1, :], 0.0)
        mix[here, lanes(x)] = total.astype(jnp.bfloat16)

    tail = pl.ds(GENES_DEV, rows - GENES_DEV)
    wait_sums = []

    def head(first, size, beginning, final):
        here = slice(first, first + size)
        spot = pl.ds(first, size)
        onehot = (slots[0:1, here] == lax.broadcasted_iota(jnp.int32, (rows, size), 0)).astype(jnp.bfloat16)
        def logits(d):
            product = jnp.dot(
                mix[here, :], hwb[at_y(d)].reshape(SIDE * group, width), preferred_element_type=jnp.float32
            )
            return product + small[at_y(d), 2:3, 0:width]

        turns = (1, 3, 0, 2) if beginning else (2, 1, 3, 0)
        ahead = logits(turns[0])
        for turn, d in enumerate(turns):
            now = ahead
            if turn + 1 < SIDE and not (beginning and turn + 1 == SIDE - 1):
                ahead = logits(turns[turn + 1])
            values = (jnp.maximum(now, 0.0) + jnp.log1p(jnp.exp(-jnp.abs(now)))).astype(jnp.bfloat16)
            out[d, here, :] = values
            acc[d] += jnp.dot(onehot, values, preferred_element_type=jnp.float32)
            if final:
                wait_sums.append(remote(acc.at[d, tail], strad_in.at[y], dev(dp=-1, dy=d), strad_in.at[at_y(-d)]))
                if d:
                    sums_out[d] = acc[d, 0:GENES_DEV].astype(jnp.bfloat16)
                    wait_sums.append(remote(sums_out.at[d], sums_in.at[y], dev(dy=d), sums_in.at[at_y(-d)]))
            if d:
                remote(out.at[d, spot], tracks.at[y, spot], dev(dy=d), tracks.at[at_y(-d), spot])
            else:
                near(out.at[0, spot], tracks.at[y, spot])
            if beginning and turn + 1 == SIDE - 1:
                for w in hw_parts[2]:
                    w()
                ahead = logits(turns[turn + 1])

    mix_ring, mix_far = [], []

    def mix_first(i):
        mix_ring.append(ring_first(mix_view(*pieces[i]), spots_x, up_x, down_x))

    def mix_second(i):
        mix_far.append(ring_second(mix_view(*pieces[i]), spots_x, up_x, down_x, mix_ring[i]))

    mixed(1)
    mix_first(0)
    acc[...] = jnp.zeros_like(acc)
    product(0, 1)
    edge_out[0] = jnp.transpose(prod[0, :, length - BLK : length])[BLK - 8 : BLK]
    wait_left = remote(edge_out.at[0], edge_in.at[0], dev(dp=1), edge_in.at[0])
    product(1, 1)
    mixed(2)
    mix_first(1)
    weights_third(hw_view, *hw_parts)
    mix_second(0)
    mixed(3)
    mix_first(2)
    weights_fourth(hw_view, *hw_parts[1:], (0, 1))
    mix_second(1)
    mixed(0)
    mix_first(3)
    weights_fourth(hw_view, *hw_parts[1:], (2,))
    for i in (0, 1, 3, 4):
        hw_parts[2][i]()
    for i, piece in enumerate(pieces):
        for w in mix_far[i]:
            w()
        head(*piece, i == 0, i == blocks - 1)
        if i + 2 < blocks:
            mix_second(i + 2)

    wait_cnt()
    for copy in started[:-19]:
        copy.wait_send()
    for w in pending[:-19]:
        w()
    for w in wait_sums:
        w()
    totals = acc[0, 0:GENES_DEV, :]
    for d in (1, 2, 3):
        totals += sums_in[at_y(-d)].astype(jnp.float32)
    strays = strad_in[0] + strad_in[1] + strad_in[2] + strad_in[3]
    counts = cnt_own[...]
    gene = lax.broadcasted_iota(jnp.int32, (GENES_DEV, width), 0)
    for s in range(STRAD):
        totals += jnp.where(gene == sm_v[0:1, s : s + 1], strays[s : s + 1, :], 0.0)
        counts += jnp.where(gene[:, 0:BLK] == sm_v[0:1, s : s + 1], cnt_in[s : s + 1, :], 0.0)
    gene_mean[...] = totals / jnp.maximum(counts, 1.0)[:, 0:1]
    finish()


def solution(mesh):
    n_pos = mesh.shape["pos"]

    def per_device(act, gain, bias, cw, hw, hb, gs, sm):
        seqs, length, ch = act.shape
        group = SIDE * ch
        width = hw.shape[1]
        rows = GENES_DEV + 8
        f32, bf16 = jnp.float32, jnp.bfloat16
        anywhere = pl.BlockSpec(memory_space=pl.ANY)
        hbm = pl.BlockSpec(memory_space=pltpu.HBM)
        vmem = pl.BlockSpec(memory_space=pltpu.VMEM)
        operands = (
            jnp.transpose(act, (0, 2, 1)),
            gain.reshape(1, ch),
            bias.reshape(1, ch),
            jnp.transpose(cw, (0, 2, 1)),
            hw.reshape(SIDE, SIDE, ch, width),
            hb.reshape(1, width),
            gs,
            sm.reshape(1, STRAD),
        )
        tracks, gene_mean = pl.pallas_call(
            functools.partial(kernel, n_pos),
            name="fused_block",
            out_shape=(
                pltpu.VMEM((seqs, length, width), bf16),
                jax.ShapeDtypeStruct((GENES_DEV, width), f32),
            ),
            in_specs=[hbm] * 8,
            out_specs=(anywhere, vmem),
            scratch_shapes=[
                pltpu.VMEM((1, ch), f32),
                pltpu.VMEM((1, ch), f32),
                pltpu.VMEM((1, width), f32),
                pltpu.VMEM((seqs, length), jnp.int32),
                pltpu.VMEM((1, STRAD), jnp.int32),
                pltpu.VMEM((SIDE, ch, length), bf16),
                pltpu.VMEM((SIDE, 8, 256), f32),
                pltpu.VMEM((SIDE, SIDE, ch, length), bf16),
                pltpu.VMEM((3, SIDE, ch, SIDE * group), bf16),
                pltpu.VMEM((SIDE, SIDE, SIDE, ch, width), bf16),
                pltpu.VMEM((3, group, length), f32),
                pltpu.VMEM((2, 8, group), f32),
                pltpu.VMEM((2, 8, group), f32),
                pltpu.VMEM((length, SIDE * group), bf16),
                pltpu.VMEM((SIDE, length, width), bf16),
                pltpu.VMEM((SIDE, rows, width), f32),
                pltpu.VMEM((SIDE, GENES_DEV, width), bf16),
                pltpu.VMEM((SIDE, GENES_DEV, width), bf16),
                pltpu.VMEM((SIDE, 8, width), f32),
                pltpu.VMEM((GENES_DEV, BLK), f32),
                pltpu.VMEM((8, BLK), f32),
                pltpu.VMEM((8, BLK), f32),
                pltpu.VMEM((8, length), jnp.int32),
                pltpu.SemaphoreType.DMA((160,)),
                pltpu.SemaphoreType.DMA((160,)),
                pltpu.SemaphoreType.DMA((24,)),
            ],
            compiler_params=pltpu.CompilerParams(
                collective_id=0, has_side_effects=True, vmem_limit_bytes=48 * 2**20
            ),
        )(*(pltpu.with_memory_space_constraint(operand, pltpu.HBM) for operand in operands))
        return tracks, gene_mean

    in_specs = (
        P(None, "pos", "trk"),
        P("trk"),
        P("trk"),
        P(None, None, "trk"),
        P(None, "trk"),
        P("trk"),
        P(None, "pos"),
        P("pos"),
    )
    out_specs = (P(None, "pos", "trk"), P("pos", "trk"))
    return jax.shard_map(per_device, mesh=mesh, in_specs=in_specs, out_specs=out_specs, check_vma=False)
```

```python
import functools

import jax
import jax.numpy as jnp
from jax import lax
from jax.experimental import pallas as pl
from jax.experimental.pallas import tpu as pltpu
from jax.sharding import PartitionSpec as P

MESH = pl.DeviceIdType.MESH
GENES_DEV = 32
STRAD = 4
SIDE = 4
BLK = 128


def kernel(
    n_pos, act, gain, bias, cw, hw, hb, gs, sm,
    tracks, gene_mean,
    gain_v, bias_v, hb_v, gs_v, sm_v, raw, small, hid, cwb, hwb, prod, edge_out, edge_in, mix, out, acc, sums_out, sums_in, strad_in, cnt_own, cnt_out, cnt_in, slots,
    send, recv, local,
):
    _, ch, length = act.shape
    group = SIDE * ch
    width = hb.shape[1]
    half = length // 2
    p = lax.axis_index("pos")
    t = lax.axis_index("trk")
    y, x = t // SIDE, t % SIDE

    def wrap(v, n):
        return lax.rem(v + n, n)

    def at_y(d):
        return wrap(y + d, SIDE)

    def at_x(d):
        return wrap(x + d, SIDE)

    def dev(dp=0, dy=0, dx=0):
        return (wrap(p + dp, n_pos), at_y(dy) * SIDE + at_x(dx))

    sibling = (p + 1 - 2 * lax.rem(p, 2), t)
    q = lax.rem(p, 4)
    q_z = lax.rem(q + 2, 4)
    q_s = q + 1 - 2 * lax.rem(q, 2)
    q_sz = lax.rem(q_s + 2, 4)

    used = [0, 0]
    started = []

    pending = []

    def once(wait):
        done = []

        def call():
            if not done:
                done.append(True)
                wait()

        pending.append(call)
        return call

    def finish():
        for w in pending:
            w()
        for copy in started[-19:]:
            copy.wait_send()

    def remote(src, dst, device, landing):
        i = used[0]
        used[0] += 1
        copy = pltpu.make_async_remote_copy(
            src_ref=src, dst_ref=dst, send_sem=send.at[i], recv_sem=recv.at[i], device_id=device, device_id_type=MESH
        )
        copy.start()
        started.append(copy)
        arrival = pltpu.make_async_remote_copy(
            src_ref=src, dst_ref=landing, send_sem=send.at[i], recv_sem=recv.at[i], device_id=device, device_id_type=MESH
        )
        return once(arrival.wait_recv)

    def near(src, dst):
        i = used[1]
        used[1] += 1
        copy = pltpu.make_async_copy(src, dst, local.at[i])
        copy.start()
        return once(copy.wait)

    wait_vectors = [near(*pair) for pair in ((gain, gain_v), (bias, bias_v), (hb, hb_v), (gs, gs_v), (sm, sm_v))]

    partners = [dev(dy=d) for d in (1, 2, 3)] + [dev(dx=d) for d in (1, 3)] + [dev(dp=d) for d in (1, -1, 2, -2)]
    partners += [dev(dp=s, dy=d) for s in (1, -1) for d in (1, 2, 3)]
    barrier = pltpu.get_barrier_semaphore()
    for partner in partners:
        pl.semaphore_signal(barrier, inc=1, device_id=partner, device_id_type=MESH)

    pl.semaphore_wait(barrier, len(partners))

    def raw_to_column(c, which):
        cols = pl.ds(c * half, half)
        return [
            remote(act.at[at_y(d), :, cols], raw.at[y, :, cols], dev(dy=d), raw.at[at_y(-d), :, cols]) for d in which
        ]

    wait_raw = [raw_to_column(0, (2,))]
    small[y, :, :] = jnp.zeros(small.shape[1:], jnp.float32)
    for w in wait_vectors:
        w()
    small[y, 0:1, 0:ch] = gain_v[...]
    small[y, 1:2, 0:ch] = bias_v[...]
    small[y, 2:3, 0:width] = hb_v[...]
    wait_small = [remote(small.at[y], small.at[y], dev(dy=d), small.at[at_y(-d)]) for d in (2, 1, 3)]
    wait_raw[0] += raw_to_column(0, (1, 3))

    def ring_first(view, spots, up, down, mine=None):
        here = view(spots[0], None)
        mine = here if mine is None else mine
        return remote(mine, here, up, view(spots[1], None)), remote(mine, here, down, view(spots[2], None))

    def ring_second(view, spots, up, down, waits):
        waits[0]()
        block = view(spots[1], 0)
        low = remote(block, block, up, view(spots[3], 0))
        waits[1]()
        block = view(spots[2], 1)
        high = remote(block, block, down, view(spots[3], 1))
        return low, high

    spots_y = (y, at_y(-1), at_y(1), at_y(2))
    spots_x = (x, at_x(-1), at_x(1), at_x(2))
    up_y, down_y, up_x, down_x = dev(dy=1), dev(dy=-1), dev(dx=1), dev(dx=-1)
    above, below = dev(dp=2), dev(dp=-2)

    def lanes(k):
        return pl.ds(pl.multiple_of(k * group, BLK), group)

    def cw_view(tap):
        def of(quarter):
            def view(k, part):
                if part is None:
                    return cwb.at[tap, k, :, lanes(quarter)]
                return cwb.at[tap, k, pl.ds(part * (ch // 2), ch // 2), lanes(quarter)]

            return view

        return of

    def hw_view(quarter):
        def view(k, part):
            if part is None:
                return hwb.at[k, quarter]
            return hwb.at[k, quarter, pl.ds(part * (SIDE // 2), SIDE // 2)]

        return view

    def to_z(view, k):
        return [
            remote(view(q)(k, 0), view(q)(k, 0), above, view(q_z)(k, 0)),
            remote(view(q)(k, 1), view(q)(k, 1), below, view(q_z)(k, 1)),
        ]

    def to_sibling(view, k, part, mine, theirs):
        return remote(view(mine)(k, part), view(mine)(k, part), sibling, view(theirs)(k, part))

    def weights_second(view, ring):
        opposite = ring_second(view(q), spots_y, up_y, down_y, ring)
        from_z, from_sibling = [], []
        for k in spots_y[1:3]:
            from_z += to_z(view, k)
            from_sibling.append(to_sibling(view, k, None, q, q_s))
        return opposite, from_z, from_sibling

    def weights_third(view, opposite, from_z, from_sibling):
        for w in opposite:
            w()
        from_z += to_z(view, spots_y[3])
        from_sibling.append(to_sibling(view, spots_y[3], None, q, q_s))

    def weights_fourth(view, from_z, from_sibling, which):
        for i in which:
            from_z[2 * i]()
            from_z[2 * i + 1]()
            from_sibling.append(to_sibling(view, spots_y[1 + i], None, q_z, q_sz))

    def hid_view(c):
        def view(k, part):
            if part is None:
                return hid.at[:, k, :, pl.ds(c * half, half)]
            return hid.at[pl.ds(part * (SIDE // 2), SIDE // 2), k, :, pl.ds(c * half, half)]

        return view

    def activate(c):
        cols = pl.ds(c * half, half)
        wait_own[c]()
        for w in wait_raw[c]:
            w()

        def channels(k, carry):
            vectors = jnp.transpose(small[k, :, 0:BLK])[0:ch]
            values = raw[k, :, cols].astype(jnp.float32) * vectors[:, 0:1] + vectors[:, 1:2]
            hid[k, x, :, cols] = jax.nn.gelu(values, approximate=True).astype(jnp.bfloat16)
            return carry

        lax.fori_loop(0, SIDE, channels, 0)
        return ring_first(hid_view(c), spots_x, up_x, down_x)

    taps = range(3)
    cw_of = [cw_view(tap) for tap in taps]

    def cw_first(tap):
        return ring_first(cw_of[tap](q), spots_y, up_y, down_y, cw.at[tap, :, lanes(q)])

    cw_ring = [cw_first(0)]
    wait_raw.append(raw_to_column(1, (2, 1, 3)))
    wait_own = [near(act.at[y, :, pl.ds(c * half, half)], raw.at[y, :, pl.ds(c * half, half)]) for c in range(2)]
    cw_ring += [cw_first(1), cw_first(2)]
    wait_cw = near(cw, cwb.at[:, y])
    wait_hw = [near(hw.at[:, k], hwb.at[y, k]) for k in range(SIDE)]

    rows = acc.shape[1]
    gene_ids = lax.broadcasted_iota(jnp.int32, (rows, length), 0)
    count = jnp.zeros((rows, 1), jnp.float32)
    for s in range(SIDE):
        count += jnp.sum((gs_v[s : s + 1, :] == gene_ids).astype(jnp.float32), axis=1, keepdims=True)
    count = jnp.broadcast_to(count, (rows, BLK))
    cnt_own[...] = count[:GENES_DEV]
    cnt_out[...] = count[GENES_DEV:]
    slots[...] = jnp.broadcast_to(gs_v[pl.ds(y, 1), :], slots.shape)
    wait_cnt = remote(cnt_out, cnt_in, dev(dp=-1), cnt_in)

    for w in wait_small:
        w()
    hid_ring = [activate(0)]
    cw_parts = [weights_second(cw_of[0], cw_ring[0])]
    hid_ring.append(activate(1))
    cw_parts.append(weights_second(cw_of[1], cw_ring[1]))
    cw_parts.append(weights_second(cw_of[2], cw_ring[2]))
    for w in wait_hw:
        w()
    hw_ring = ring_first(hw_view(q), spots_y, up_y, down_y)
    weights_fourth(cw_of[0], *cw_parts[0][1:], (0, 1))
    weights_third(cw_of[0], *cw_parts[0])
    hid_far = [ring_second(hid_view(0), spots_x, up_x, down_x, hid_ring[0])]
    weights_third(cw_of[1], *cw_parts[1])
    weights_third(cw_of[2], *cw_parts[2])
    weights_fourth(cw_of[1], *cw_parts[1][1:], (0, 1))
    weights_fourth(cw_of[2], *cw_parts[2][1:], (0, 1))
    weights_fourth(cw_of[0], *cw_parts[0][1:], (2,))
    hid_far.append(ring_second(hid_view(1), spots_x, up_x, down_x, hid_ring[1]))
    weights_fourth(cw_of[1], *cw_parts[1][1:], (2,))
    weights_fourth(cw_of[2], *cw_parts[2][1:], (2,))

    def product(tap, c):
        cols = pl.ds(c * half, half)
        wait_cw()
        for w in (*cw_parts[tap][2], *hid_far[c]):
            w()
        prod[tap, :, cols] = jnp.dot(
            cwb[tap].reshape(group, SIDE * group),
            hid[:, :, :, cols].reshape(SIDE * group, half),
            preferred_element_type=jnp.float32,
        )

    product(0, 0)
    product(1, 0)
    hw_parts = weights_second(hw_view, hw_ring)
    product(2, 0)
    edge_out[1] = jnp.transpose(prod[2, :, 0:BLK])[0:8]
    wait_right = remote(edge_out.at[1], edge_in.at[1], dev(dp=-1), edge_in.at[1])
    product(2, 1)

    def mix_view(first, size):
        def view(k, part):
            if part is None:
                return mix.at[pl.ds(first, size), lanes(k)]
            return mix.at[pl.ds(first + part * (size // 2), size // 2), lanes(k)]

        return view

    lane = lax.broadcasted_iota(jnp.int32, (group, BLK), 1)
    row = lax.broadcasted_iota(jnp.int32, (BLK, group), 0)
    blocks = length // BLK
    order = list(range(1, blocks)) + [0]
    pieces = [(b * BLK, BLK) for b in order]

    def mixed(b):
        here = slice(b * BLK, (b + 1) * BLK)
        before = pltpu.roll(prod[0, :, here], 1, 1)
        if b > 0:
            other = pltpu.roll(prod[0, :, (b - 1) * BLK : b * BLK], 1, 1)
        else:
            other = jnp.zeros_like(before)
        total = prod[1, :, here] + jnp.where(lane == 0, other, before)
        after = pltpu.roll(prod[2, :, here], BLK - 1, 1)
        if b < blocks - 1:
            other = pltpu.roll(prod[2, :, (b + 1) * BLK : (b + 2) * BLK], BLK - 1, 1)
        else:
            other = jnp.zeros_like(after)
        total += jnp.where(lane == BLK - 1, other, after)
        total += raw[:, :, here].reshape(group, BLK).astype(jnp.float32)
        total = jnp.transpose(total)
        if b == 0:
            wait_left()
            total += jnp.where((row == 0) & (p > 0), edge_in[0, 7:8, :], 0.0)
        if b == blocks - 1:
            wait_right()
            total += jnp.where((row == BLK - 1) & (p < n_pos - 1), edge_in[1, 0:1, :], 0.0)
        mix[here, lanes(x)] = total.astype(jnp.bfloat16)

    tail = pl.ds(GENES_DEV, rows - GENES_DEV)
    wait_sums = []

    def head(first, size, beginning, final):
        here = slice(first, first + size)
        spot = pl.ds(first, size)
        onehot = (slots[0:1, here] == lax.broadcasted_iota(jnp.int32, (rows, size), 0)).astype(jnp.bfloat16)
        def logits(d):
            product = jnp.dot(
                mix[here, :], hwb[at_y(d)].reshape(SIDE * group, width), preferred_element_type=jnp.float32
            )
            return product + small[at_y(d), 2:3, 0:width]

        turns = (1, 3, 0, 2) if beginning else (2, 1, 3, 0)
        ahead = logits(turns[0])
        for turn, d in enumerate(turns):
            now = ahead
            if turn + 1 < SIDE and not (beginning and turn + 1 == SIDE - 1):
                ahead = logits(turns[turn + 1])
            values = (jnp.maximum(now, 0.0) + jnp.log1p(jnp.exp(-jnp.abs(now)))).astype(jnp.bfloat16)
            out[d, here, :] = values
            acc[d] += jnp.dot(onehot, values, preferred_element_type=jnp.float32)
            if final:
                wait_sums.append(remote(acc.at[d, tail], strad_in.at[y], dev(dp=-1, dy=d), strad_in.at[at_y(-d)]))
                if d:
                    sums_out[d] = acc[d, 0:GENES_DEV].astype(jnp.bfloat16)
                    wait_sums.append(remote(sums_out.at[d], sums_in.at[y], dev(dy=d), sums_in.at[at_y(-d)]))
            if d:
                remote(out.at[d, spot], tracks.at[y, spot], dev(dy=d), tracks.at[at_y(-d), spot])
            else:
                near(out.at[0, spot], tracks.at[y, spot])
            if beginning and turn + 1 == SIDE - 1:
                for w in hw_parts[2]:
                    w()
                ahead = logits(turns[turn + 1])

    mix_ring, mix_far = [], []

    def mix_first(i):
        mix_ring.append(ring_first(mix_view(*pieces[i]), spots_x, up_x, down_x))

    def mix_second(i):
        mix_far.append(ring_second(mix_view(*pieces[i]), spots_x, up_x, down_x, mix_ring[i]))

    mixed(1)
    mix_first(0)
    acc[...] = jnp.zeros_like(acc)
    product(0, 1)
    edge_out[0] = jnp.transpose(prod[0, :, length - BLK : length])[BLK - 8 : BLK]
    wait_left = remote(edge_out.at[0], edge_in.at[0], dev(dp=1), edge_in.at[0])
    product(1, 1)
    mixed(2)
    mix_first(1)
    mixed(3)
    mix_first(2)
    weights_third(hw_view, *hw_parts)
    mix_second(0)
    mixed(0)
    mix_first(3)
    weights_fourth(hw_view, *hw_parts[1:], (0, 1))
    mix_second(1)
    weights_fourth(hw_view, *hw_parts[1:], (2,))
    for i in (0, 1, 3, 4):
        hw_parts[2][i]()
    mix_second(2)
    for i, piece in enumerate(pieces):
        for w in mix_far[i]:
            w()
        head(*piece, i == 0, i == blocks - 1)
        if i == 0:
            mix_second(3)

    wait_cnt()
    for copy in started[:-19]:
        copy.wait_send()
    for w in pending[:-19]:
        w()
    for w in wait_sums:
        w()
    totals = acc[0, 0:GENES_DEV, :]
    for d in (1, 2, 3):
        totals += sums_in[at_y(-d)].astype(jnp.float32)
    strays = strad_in[0] + strad_in[1] + strad_in[2] + strad_in[3]
    counts = cnt_own[...]
    gene = lax.broadcasted_iota(jnp.int32, (GENES_DEV, width), 0)
    for s in range(STRAD):
        totals += jnp.where(gene == sm_v[0:1, s : s + 1], strays[s : s + 1, :], 0.0)
        counts += jnp.where(gene[:, 0:BLK] == sm_v[0:1, s : s + 1], cnt_in[s : s + 1, :], 0.0)
    gene_mean[...] = totals / jnp.maximum(counts, 1.0)[:, 0:1]
    finish()


def solution(mesh):
    n_pos = mesh.shape["pos"]

    def per_device(act, gain, bias, cw, hw, hb, gs, sm):
        seqs, length, ch = act.shape
        group = SIDE * ch
        width = hw.shape[1]
        rows = GENES_DEV + 8
        f32, bf16 = jnp.float32, jnp.bfloat16
        anywhere = pl.BlockSpec(memory_space=pl.ANY)
        hbm = pl.BlockSpec(memory_space=pltpu.HBM)
        vmem = pl.BlockSpec(memory_space=pltpu.VMEM)
        operands = (
            jnp.transpose(act, (0, 2, 1)),
            gain.reshape(1, ch),
            bias.reshape(1, ch),
            jnp.transpose(cw, (0, 2, 1)),
            hw.reshape(SIDE, SIDE, ch, width),
            hb.reshape(1, width),
            gs,
            sm.reshape(1, STRAD),
        )
        tracks, gene_mean = pl.pallas_call(
            functools.partial(kernel, n_pos),
            name="fused_block",
            out_shape=(
                pltpu.VMEM((seqs, length, width), bf16),
                jax.ShapeDtypeStruct((GENES_DEV, width), f32),
            ),
            in_specs=[hbm] * 8,
            out_specs=(anywhere, vmem),
            scratch_shapes=[
                pltpu.VMEM((1, ch), f32),
                pltpu.VMEM((1, ch), f32),
                pltpu.VMEM((1, width), f32),
                pltpu.VMEM((seqs, length), jnp.int32),
                pltpu.VMEM((1, STRAD), jnp.int32),
                pltpu.VMEM((SIDE, ch, length), bf16),
                pltpu.VMEM((SIDE, 8, 256), f32),
                pltpu.VMEM((SIDE, SIDE, ch, length), bf16),
                pltpu.VMEM((3, SIDE, ch, SIDE * group), bf16),
                pltpu.VMEM((SIDE, SIDE, SIDE, ch, width), bf16),
                pltpu.VMEM((3, group, length), f32),
                pltpu.VMEM((2, 8, group), f32),
                pltpu.VMEM((2, 8, group), f32),
                pltpu.VMEM((length, SIDE * group), bf16),
                pltpu.VMEM((SIDE, length, width), bf16),
                pltpu.VMEM((SIDE, rows, width), f32),
                pltpu.VMEM((SIDE, GENES_DEV, width), bf16),
                pltpu.VMEM((SIDE, GENES_DEV, width), bf16),
                pltpu.VMEM((SIDE, 8, width), f32),
                pltpu.VMEM((GENES_DEV, BLK), f32),
                pltpu.VMEM((8, BLK), f32),
                pltpu.VMEM((8, BLK), f32),
                pltpu.VMEM((8, length), jnp.int32),
                pltpu.SemaphoreType.DMA((160,)),
                pltpu.SemaphoreType.DMA((160,)),
                pltpu.SemaphoreType.DMA((24,)),
            ],
            compiler_params=pltpu.CompilerParams(
                collective_id=0, has_side_effects=True, vmem_limit_bytes=48 * 2**20
            ),
        )(*(pltpu.with_memory_space_constraint(operand, pltpu.HBM) for operand in operands))
        return tracks, gene_mean

    in_specs = (
        P(None, "pos", "trk"),
        P("trk"),
        P("trk"),
        P(None, None, "trk"),
        P(None, "trk"),
        P("trk"),
        P(None, "pos"),
        P("pos"),
    )
    out_specs = (P(None, "pos", "trk"), P("pos", "trk"))
    return jax.shard_map(per_device, mesh=mesh, in_specs=in_specs, out_specs=out_specs, check_vma=False)
```
